32 devices in a mesh: grp: 4 (over y, x), seq: 8 (over z, core).
Axes of the slice: x: 2, y: 2, z: 4, core: 2. Of those that a mesh axis runs over, the one named last changes fastest.
Arguments:
- thinker_input: bfloat16 [4, 32, 3584], P(None, 'grp'), as said below
- thinker_gain: float32 [3584], replicated, may hold values from 0.25 to 1.75
- thinker_qkv: bfloat16 [3584, 4608], P('seq'), may hold values from -0.09375 to 0.09375
- thinker_out: bfloat16 [3584, 3584], P('seq'), may hold values from -0.09375 to 0.09375
- talker_proj: bfloat16 [3584, 896], P('seq'), may hold values from -0.09375 to 0.09375
- code_table: bfloat16 [8448, 896], P('seq'), may hold values from -6 to 6
- talker_gain: float32 [896], replicated, may hold values from 0.25 to 1.75
- talker_qkv: bfloat16 [896, 2560], replicated, may hold values from -0.1875 to 0.1875
- talker_out: bfloat16 [1536, 896], replicated, may hold values from -0.15625 to 0.15625
- text_keys: bfloat16 [32, 1024, 512], P('grp', 'seq'), as said below
- text_values: bfloat16 [32, 1024, 512], P('grp', 'seq'), may hold values from -72 to 72
- audio_keys: bfloat16 [32, 1024, 512], P('grp', 'seq'), as said below
- audio_values: bfloat16 [32, 1024, 512], P('grp', 'seq'), may hold values from -72 to 72
- text_len: int32 [32], P('grp'), may hold values from 2 to 1024
- audio_len: int32 [32], P('grp'), may hold values from 2 to 1024
- text_pos: int32 [32, 4], P('grp'), may hold values from 0 to 1027
- audio_pos: int32 [32, 4], P('grp'), may hold values from 0 to 1027
- code_ids: int32 [32, 4], P('grp'), may hold values from 0 to 8447
Outputs:
- thinker_hidden: bfloat16 [4, 32, 3584], P(None, 'grp')
- talker_hidden: bfloat16 [4, 32, 896], P(None, 'grp', 'seq')
The draws below stay inside these ranges and needn't reach their ends.
Inputs may be any that keep to these rules, and one draw needn't show every extreme that they name: Cache positions 0 .. text_len - 1 of a conversation are live. Cache positions 0 .. audio_len - 1 of a conversation are live. `thinker_input`: real-valued, of order one per feature. `text_keys`: real-valued. `audio_keys`: real-valued.
All inputs are finite; a program needn't handle non-finite values.
Results may differ from the reference program's by a relative error of at most 0.028.
Values may be sent and summed in bfloat16 or wider, within the bound.
A program may use at most 128 MiB of HBM per device.

```python
import math
import jax
import jax.numpy as jnp
import numpy as np
from jax import lax

D = 3584
HQ = 28
HK = 4
HD = 128
TD = 896
AHQ = 12
AHK = 4
AHD = 128
VOCAB = 8448
STEPS = 4
B = 32
TEXT_MAX = 1024
AUDIO_MAX = 1024


def draw_thinker_input(key, part):
    first, second = jax.random.split(jax.random.fold_in(key, 11), 2)
    base = jax.random.normal(first, (STEPS, B, D), jnp.float32)
    columns = jnp.exp(jnp.linspace(jnp.log(0.6), jnp.log(1.8), D))
    rows = jnp.exp(jax.random.uniform(second, (1, B, 1), jnp.float32, jnp.log(0.3), jnp.log(3.0)))
    return jnp.clip(base * rows * columns, -30.0, 30.0).astype(jnp.bfloat16)


def cache_keys(key, batch, count, width):
    first = jax.random.fold_in(key, 0)
    base = 1.5 * jax.random.normal(first, (batch, count, width), jnp.float32)
    return base.astype(jnp.bfloat16)


def draw_text_keys(key, part):
    return cache_keys(jax.random.fold_in(key, 21), B, TEXT_MAX, HK * HD)


def draw_audio_keys(key, part):
    return cache_keys(jax.random.fold_in(key, 31), B, AUDIO_MAX, AHK * AHD)


def touch_ends(drawn, key, low, largest):
    longest = drawn.shape.index(max(drawn.shape))
    spots = []
    for shift in (0, 1):
        where = [jax.random.randint(jax.random.fold_in(key, axis), (), 0, length) for axis, length in enumerate(drawn.shape)]
        where[longest] = (where[longest] + shift) % drawn.shape[longest]
        spots.append(tuple(where))
    return drawn.at[spots[0]].set(low).at[spots[1]].set(largest)


def block_levels(stream_key, shape, cuts, smallest, top_value):
    def one(axis_at, blocks):
        steps = jax.random.uniform(jax.random.fold_in(jax.random.fold_in(stream_key, 6), axis_at), (blocks,), jnp.float32, smallest / len(cuts), top_value / len(cuts))
        return jnp.repeat(jnp.exp(steps), shape[axis_at] // blocks).reshape((-1,) + (1,) * (len(shape) - axis_at - 1))

    gain = one(*cuts[0])
    for cut in cuts[1:]:
        gain = gain * one(*cut)
    return gain


def rank_bounds(amount, slope):
    loads = [(1 << 20) // math.isqrt(rank ** slope) + 1 for rank in range(1, amount + 1)]
    deviation = 1 + sum(loads) // (1 << 30)
    return np.cumsum(np.array([max(1, weight // deviation) for weight in loads]))


def ranked(stream_key, dims, count, lean):
    listing = rank_bounds(count, lean)
    ticket = jax.random.randint(jax.random.fold_in(stream_key, 1), dims, 0, int(listing[count - 1]))
    grade = jnp.searchsorted(jnp.asarray(listing, jnp.int32), ticket, side="right")
    return jax.random.permutation(jax.random.fold_in(stream_key, 2), count)[grade].astype(jnp.int32)


def normal_values(stream_key, extent, scale, reach, cuts=(), held_as=jnp.bfloat16):
    entries = scale * jax.random.normal(stream_key, extent, jnp.float32)
    if cuts:
        entries = entries * block_levels(stream_key, extent, cuts, -0.22, 0.18)
    return jnp.clip(entries, -reach, reach).astype(held_as)


def setup_inputs(seed: int = 0) -> dict:
    key_of = jax.random.split(jax.random.key(seed), 19)
    return {
        "thinker_input": draw_thinker_input(jax.random.fold_in(key_of[18], 71), 0),
        "thinker_gain": jnp.clip(1.0 + 0.15 * jax.random.normal(key_of[1], (D,), jnp.float32), 0.25, 1.75),
        "thinker_qkv": normal_values(key_of[2], (D, D + 2 * HK * HD), D ** -0.5, 0.09375, ((0, 8),)),
        "thinker_out": normal_values(key_of[3], (D, D), D ** -0.5, 0.09375, ((0, 8),)),
        "talker_proj": normal_values(key_of[4], (D, TD), D ** -0.5, 0.09375, ((0, 8),)),
        "code_table": normal_values(key_of[5], (VOCAB, TD), 1.0, 6.0, ((0, 8),)),
        "talker_gain": jnp.clip(1.0 + 0.15 * jax.random.normal(key_of[6], (TD,), jnp.float32), 0.25, 1.75),
        "talker_qkv": normal_values(key_of[7], (TD, AHQ * AHD + 2 * AHK * AHD), TD ** -0.5, 0.1875),
        "talker_out": normal_values(key_of[8], (AHQ * AHD, TD), (AHQ * AHD) ** -0.5, 0.15625),
        "text_keys": draw_text_keys(jax.random.fold_in(key_of[18], 71), 0),
        "text_values": normal_values(key_of[10], (B, TEXT_MAX, HK * HD), 12.0, 72.0, ((0, 4), (1, 8))),
        "audio_keys": draw_audio_keys(jax.random.fold_in(key_of[18], 71), 0),
        "audio_values": normal_values(key_of[12], (B, AUDIO_MAX, AHK * AHD), 12.0, 72.0, ((0, 4), (1, 8))),
        "text_len": touch_ends(jax.random.randint(key_of[13], (B,), 2, TEXT_MAX + 1), jax.random.fold_in(key_of[13], 1), 2, TEXT_MAX).astype(jnp.int32),
        "audio_len": touch_ends(jax.random.randint(key_of[14], (B,), 2, AUDIO_MAX + 1), jax.random.fold_in(key_of[14], 1), 2, AUDIO_MAX).astype(jnp.int32),
        "text_pos": touch_ends(jax.random.randint(key_of[15], (B, STEPS), 0, TEXT_MAX + STEPS), jax.random.fold_in(key_of[15], 1), 0, (TEXT_MAX + STEPS) - 1).astype(jnp.int32),
        "audio_pos": touch_ends(jax.random.randint(key_of[16], (B, STEPS), 0, AUDIO_MAX + STEPS), jax.random.fold_in(key_of[16], 1), 0, (AUDIO_MAX + STEPS) - 1).astype(jnp.int32),
        "code_ids": touch_ends(ranked(key_of[17], (B, STEPS), VOCAB, 2), jax.random.fold_in(key_of[17], 3), 0, VOCAB - 1).astype(jnp.int32),
    }


EPSILON = 1e-06
THETA = 1000000.0
NEGATIVE = -1e+30

def rotate(vectors, positions):
    width = vectors.shape[-1]
    half = width // 2
    freqs = jnp.exp(jnp.arange(half).astype(jnp.float32) * (-2.0 * jnp.log(jnp.float32(THETA)) / width))
    angles = positions.astype(jnp.float32)[:, None] * freqs[None, :]
    cosine = jnp.cos(angles)[:, None, :]
    sine = jnp.sin(angles)[:, None, :]
    first = vectors[..., :half]
    second = vectors[..., half:]
    return jnp.concatenate([first * cosine - second * sine, second * cosine + first * sine], axis=-1)

def attend_all(query, keys, values, new_keys, new_values, lengths, step):
    heads, group, width = query.shape[1:]
    steps = new_keys.shape[1]
    scale = width ** (-0.5)
    fresh_live = jnp.arange(steps) <= step

    def single(item):
        quest, key_cache, value_cache, key_new, value_new, length = item
        count = key_cache.shape[0]
        key_four = key_cache.reshape(count, heads, width).astype(jnp.float32)
        value_four = value_cache.reshape(count, heads, width).astype(jnp.float32)
        quest_wide = quest.astype(jnp.float32)
        cached = jnp.einsum('kgd,tkd->kgt', quest_wide, key_four) * scale
        fresh = jnp.einsum('kgd,skd->kgs', quest_wide, key_new.astype(jnp.float32)) * scale
        live = jnp.arange(count) < length
        cached = jnp.where(live[None, None, :], cached, NEGATIVE)
        fresh = jnp.where(fresh_live[None, None, :], fresh, NEGATIVE)
        peak = jnp.maximum(cached.max(-1), fresh.max(-1))
        weight_cached = jnp.where(live[None, None, :], jnp.exp(cached - peak[..., None]), 0.0)
        weight_fresh = jnp.where(fresh_live[None, None, :], jnp.exp(fresh - peak[..., None]), 0.0)
        total = weight_cached.sum(-1) + weight_fresh.sum(-1)
        narrow_cached = lax.optimization_barrier(weight_cached.astype(jnp.bfloat16)).astype(jnp.float32)
        narrow_fresh = lax.optimization_barrier(weight_fresh.astype(jnp.bfloat16)).astype(jnp.float32)
        summed = jnp.einsum('kgt,tkd->kgd', narrow_cached, value_four)
        summed = summed + jnp.einsum('kgs,skd->kgd', narrow_fresh, value_new.astype(jnp.float32))
        return (summed / total[..., None]).reshape(heads * group * width).astype(jnp.bfloat16)
    return lax.map(single, (query, keys, values, new_keys, new_values, lengths))

def reference(thinker_input, thinker_gain, thinker_qkv, thinker_out, talker_proj, code_table, talker_gain, talker_qkv, talker_out, text_keys, text_values, audio_keys, audio_values, text_len, audio_len, text_pos, audio_pos, code_ids):
    batch = thinker_input.shape[1]
    text_kv = HK * HD
    audio_q = AHQ * AHD
    audio_kv = AHK * AHD
    new_text_keys = jnp.zeros((batch, STEPS, HK, HD), jnp.bfloat16)
    new_text_values = jnp.zeros((batch, STEPS, HK, HD), jnp.bfloat16)
    new_audio_keys = jnp.zeros((batch, STEPS, AHK, AHD), jnp.bfloat16)
    new_audio_values = jnp.zeros((batch, STEPS, AHK, AHD), jnp.bfloat16)
    thinker_rows = []
    talker_rows = []
    for step in range(STEPS):
        inputs = thinker_input[step].astype(jnp.float32)
        scaled = (inputs * thinker_gain).astype(jnp.bfloat16)
        factor = lax.rsqrt(lax.optimization_barrier(jnp.sum(inputs * inputs, axis=-1)) / D + EPSILON)[:, None]
        projected = jnp.dot(scaled, thinker_qkv, preferred_element_type=jnp.float32) * factor
        query = rotate(projected[:, :D].reshape(batch, HQ, HD), text_pos[:, step]).astype(jnp.bfloat16)
        key = rotate(projected[:, D:D + text_kv].reshape(batch, HK, HD), text_pos[:, step]).astype(jnp.bfloat16)
        value = projected[:, D + text_kv:].reshape(batch, HK, HD).astype(jnp.bfloat16)
        new_text_keys = new_text_keys.at[:, step].set(key)
        new_text_values = new_text_values.at[:, step].set(value)
        attended = attend_all(query.reshape(batch, HK, HQ // HK, HD), text_keys, text_values, new_text_keys, new_text_values, text_len, step)
        hidden = (inputs + jnp.dot(attended, thinker_out, preferred_element_type=jnp.float32)).astype(jnp.bfloat16)
        thinker_rows.append(hidden)
        talker_in = code_table[code_ids[:, step]].astype(jnp.float32) + jnp.dot(hidden, talker_proj, preferred_element_type=jnp.float32)
        normed = (talker_in * lax.rsqrt(lax.optimization_barrier(jnp.sum(talker_in * talker_in, axis=-1, keepdims=True)) / TD + EPSILON) * talker_gain).astype(jnp.bfloat16)
        spoken = jnp.dot(normed, talker_qkv, preferred_element_type=jnp.float32)
        audio_query = rotate(spoken[:, :audio_q].reshape(batch, AHQ, AHD), audio_pos[:, step]).astype(jnp.bfloat16)
        audio_key = rotate(spoken[:, audio_q:audio_q + audio_kv].reshape(batch, AHK, AHD), audio_pos[:, step]).astype(jnp.bfloat16)
        audio_value = spoken[:, audio_q + audio_kv:].reshape(batch, AHK, AHD).astype(jnp.bfloat16)
        new_audio_keys = new_audio_keys.at[:, step].set(audio_key)
        new_audio_values = new_audio_values.at[:, step].set(audio_value)
        heard = attend_all(audio_query.reshape(batch, AHK, AHQ // AHK, AHD), audio_keys, audio_values, new_audio_keys, new_audio_values, audio_len, step)
        talker_rows.append((talker_in + jnp.dot(heard, talker_out, preferred_element_type=jnp.float32)).astype(jnp.bfloat16))
    return (jnp.stack(thinker_rows), jnp.stack(talker_rows))
```

```python
import jax
import jax.numpy as jnp
from jax import lax
from jax.sharding import PartitionSpec as P

D = 3584
HQ = 28
HK = 4
HD = 128
TD = 896
AHQ = 12
AHK = 4
AHD = 128


EPSILON = 1e-06
THETA = 1000000.0
NEGATIVE = -1e30


def rotate(vectors, positions):
    width = vectors.shape[-1]
    half = width // 2
    freqs = jnp.exp(
        jnp.arange(half).astype(jnp.float32) * (-2.0 * jnp.log(jnp.float32(THETA)) / width)
    )
    angles = positions.astype(jnp.float32)[:, None] * freqs[None, :]
    cosine = jnp.cos(angles)[:, None, :]
    sine = jnp.sin(angles)[:, None, :]
    first = vectors[..., :half]
    second = vectors[..., half:]
    return jnp.concatenate(
        [first * cosine - second * sine, second * cosine + first * sine], axis=-1
    )


def attend(query, keys, values, new_keys, new_values, live, first):
    batch, steps, heads, group, width = query.shape
    count = keys.shape[1]
    scale = width ** (-0.5)
    key_four = keys.reshape(batch, count, heads, width)
    value_four = values.reshape(batch, count, heads, width)
    cached = (
        jnp.einsum("bskgd,btkd->bksgt", query, key_four, preferred_element_type=jnp.float32) * scale
    )
    fresh = (
        jnp.einsum("bskgd,bukd->bksgu", query, new_keys, preferred_element_type=jnp.float32) * scale
    )
    order = jnp.arange(steps)
    live_mask = live[:, None, None, None, :]
    fresh_mask = ((order[None, :] <= order[:, None]) & first)[None, None, :, None, :]
    cached = jnp.where(live_mask, cached, NEGATIVE)
    fresh = jnp.where(fresh_mask, fresh, NEGATIVE)
    peak = lax.pmax(jnp.maximum(cached.max(-1), fresh.max(-1)), "seq")
    weight_cached = jnp.where(live_mask, jnp.exp(cached - peak[..., None]), 0.0)
    weight_fresh = jnp.where(fresh_mask, jnp.exp(fresh - peak[..., None]), 0.0)
    total = weight_cached.sum(-1) + weight_fresh.sum(-1)
    summed = jnp.einsum(
        "bksgt,btkd->bksgd",
        weight_cached.astype(jnp.bfloat16),
        value_four,
        preferred_element_type=jnp.float32,
    ) + jnp.einsum(
        "bksgu,bukd->bksgd",
        weight_fresh.astype(jnp.bfloat16),
        new_values,
        preferred_element_type=jnp.float32,
    )
    total, summed = lax.psum((total, summed), "seq")
    out = (summed / total[..., None]).astype(jnp.bfloat16)
    return out.transpose(2, 0, 1, 3, 4).reshape(steps * batch, heads * group * width)


def body(
    thinker_input,
    thinker_gain,
    thinker_qkv,
    thinker_out,
    talker_proj,
    code_table,
    talker_gain,
    talker_qkv,
    talker_out,
    text_keys,
    text_values,
    audio_keys,
    audio_values,
    text_len,
    audio_len,
    text_pos,
    audio_pos,
    code_ids,
):
    steps, batch = thinker_input.shape[:2]
    rows = steps * batch
    index = lax.axis_index("seq")
    shards = lax.axis_size("seq")
    text_kv = HK * HD
    audio_q = AHQ * AHD
    audio_kv = AHK * AHD

    def live_of(cache, lengths):
        count = cache.shape[1]
        return (index * count + jnp.arange(count))[None, :] < lengths[:, None]

    def by_batch(heads):
        return heads.reshape((steps, batch) + heads.shape[1:]).swapaxes(0, 1)

    table_rows = code_table.shape[0]
    table_ids = index * table_rows + jnp.arange(table_rows)
    talker_cols = talker_out.shape[1] // shards
    out_slice = lax.dynamic_slice_in_dim(talker_out, index * talker_cols, talker_cols, 1)
    text_at = text_pos.T.reshape(rows)
    audio_at = audio_pos.T.reshape(rows)
    ids = code_ids.T.reshape(rows)

    inputs = thinker_input.reshape(rows, D).astype(jnp.float32)
    scaled = (inputs * thinker_gain).astype(jnp.bfloat16)
    n = thinker_qkv.shape[0]
    mine = lax.dynamic_slice_in_dim(scaled, index * n, n, 1)
    projected = lax.psum(jnp.dot(mine, thinker_qkv, preferred_element_type=jnp.float32), "seq")
    projected = projected * lax.rsqrt(jnp.sum(inputs * inputs, axis=-1) / D + EPSILON)[:, None]
    query = rotate(projected[:, :D].reshape(rows, HQ, HD), text_at).astype(jnp.bfloat16)
    key = rotate(projected[:, D : D + text_kv].reshape(rows, HK, HD), text_at).astype(jnp.bfloat16)
    value = projected[:, D + text_kv :].reshape(rows, HK, HD).astype(jnp.bfloat16)
    attended = attend(
        by_batch(query.reshape(rows, HK, HQ // HK, HD)),
        text_keys,
        text_values,
        by_batch(key),
        by_batch(value),
        live_of(text_keys, text_len),
        index == 0,
    )
    n = thinker_out.shape[0]
    mine = lax.dynamic_slice_in_dim(attended, index * n, n, 1)
    contribution = lax.psum(jnp.dot(mine, thinker_out, preferred_element_type=jnp.float32), "seq")
    hidden = (inputs + contribution).astype(jnp.bfloat16)
    picked = (ids[:, None] == table_ids[None, :]).astype(jnp.bfloat16)
    n = talker_proj.shape[0]
    mine = lax.dynamic_slice_in_dim(hidden, index * n, n, 1)
    talker_in = lax.psum(
        jnp.dot(mine, talker_proj, preferred_element_type=jnp.float32)
        + jnp.dot(picked, code_table, preferred_element_type=jnp.float32),
        "seq",
    )
    normed = (
        talker_in
        * lax.rsqrt(jnp.sum(talker_in * talker_in, axis=-1, keepdims=True) / TD + EPSILON)
        * talker_gain
    ).astype(jnp.bfloat16)
    spoken = jnp.dot(normed, talker_qkv, preferred_element_type=jnp.float32)
    query = rotate(spoken[:, :audio_q].reshape(rows, AHQ, AHD), audio_at).astype(jnp.bfloat16)
    key = rotate(
        spoken[:, audio_q : audio_q + audio_kv].reshape(rows, AHK, AHD), audio_at
    ).astype(jnp.bfloat16)
    value = spoken[:, audio_q + audio_kv :].reshape(rows, AHK, AHD).astype(jnp.bfloat16)
    heard = attend(
        by_batch(query.reshape(rows, AHK, AHQ // AHK, AHD)),
        audio_keys,
        audio_values,
        by_batch(key),
        by_batch(value),
        live_of(audio_keys, audio_len),
        index == 0,
    )
    residual = lax.dynamic_slice_in_dim(talker_in, index * talker_cols, talker_cols, 1)
    spoken_out = residual + jnp.dot(heard, out_slice, preferred_element_type=jnp.float32)
    return (
        hidden.reshape(steps, batch, D),
        spoken_out.astype(jnp.bfloat16).reshape(steps, batch, talker_cols),
    )


def solution(mesh):
    return jax.shard_map(
        body,
        mesh=mesh,
        in_specs=(
            P(None, "grp", None),
            P(),
            P("seq", None),
            P("seq", None),
            P("seq", None),
            P("seq", None),
            P(),
            P(),
            P(),
            P("grp", "seq", None),
            P("grp", "seq", None),
            P("grp", "seq", None),
            P("grp", "seq", None),
            P("grp"),
            P("grp"),
            P("grp", None),
            P("grp", None),
            P("grp", None),
        ),
        out_specs=(P(None, "grp", None), P(None, "grp", "seq")),
        check_vma=False,
    )
```

```python
import functools

import jax
import jax.numpy as jnp
from jax import lax
from jax.experimental import pallas as pl
from jax.experimental.pallas import tpu as pltpu
from jax.sharding import PartitionSpec as P

D = 3584
HQ = 28
HK = 4
HD = 128
TD = 896
AHQ = 12
AHK = 4
AHD = 128


EPSILON = 1e-06
THETA = 1000000.0
NEGATIVE = -1e30


def rotate(vectors, positions):
    width = vectors.shape[-1]
    half = width // 2
    freqs = jnp.exp(
        jnp.arange(half).astype(jnp.float32) * (-2.0 * jnp.log(jnp.float32(THETA)) / width)
    )
    angles = positions.astype(jnp.float32)[:, None] * freqs[None, :]
    cosine = jnp.cos(angles)[:, None, :]
    sine = jnp.sin(angles)[:, None, :]
    first = vectors[..., :half]
    second = vectors[..., half:]
    return jnp.concatenate(
        [first * cosine - second * sine, second * cosine + first * sine], axis=-1
    )


LANES = 128


def greet(n, me):
    barrier = pltpu.get_barrier_semaphore()
    for off in range(1, n):
        pl.semaphore_signal(
            barrier,
            inc=1,
            device_id={"seq": lax.rem(me + off, n)},
            device_id_type=pl.DeviceIdType.MESH,
        )
    return barrier


def remote(n, me, off, src, dst, send_sem, recv_sem):
    return pltpu.make_async_remote_copy(
        src_ref=src,
        dst_ref=dst,
        send_sem=send_sem.at[off - 1],
        recv_sem=recv_sem.at[off - 1],
        device_id={"seq": lax.rem(me + off, n)},
        device_id_type=pl.DeviceIdType.MESH,
    )


def sum_kernel(n, per, x_ref, o_ref, sent, landed, whole, send_one, recv_one, send_two, recv_two):
    me = lax.axis_index("seq")
    barrier = greet(n, me)
    blocks = x_ref.shape[1] // LANES
    for j in range(blocks):
        sent[j] = x_ref[:, j * LANES : (j + 1) * LANES].astype(sent.dtype)
    for j in range(blocks, n * per):
        sent[j] = jnp.zeros(sent.shape[1:], sent.dtype)
    pl.semaphore_wait(barrier, n - 1)
    out = []
    for off in range(1, n):
        part = pl.ds(lax.rem(me + off, n) * per, per)
        out.append(remote(n, me, off, sent.at[part], landed.at[off - 1], send_one, recv_one))
        out[-1].start()
    mine = pl.ds(me * per, per)
    total = sent[mine].astype(jnp.float32)
    for off in range(1, n):
        out[off - 1].wait_recv()
        total = total + landed[off - 1].astype(jnp.float32)
    whole[mine] = total.astype(whole.dtype)
    back = []
    for off in range(1, n):
        back.append(remote(n, me, off, whole.at[mine], whole.at[mine], send_two, recv_two))
        back[-1].start()
    for copy in out:
        copy.wait_send()
    for copy in back:
        copy.wait_recv()
    for j in range(blocks):
        o_ref[:, j * LANES : (j + 1) * LANES] = whole[j].astype(o_ref.dtype)
    for copy in back:
        copy.wait_send()


def sum_over(x, n, ident):
    rows, columns = x.shape
    per = -(-(columns // LANES) // n)
    vmem = pl.BlockSpec(memory_space=pltpu.VMEM)
    dma = pltpu.SemaphoreType.DMA((n - 1,))
    return pl.pallas_call(
        functools.partial(sum_kernel, n, per),
        out_shape=jax.ShapeDtypeStruct(x.shape, jnp.float32),
        in_specs=[vmem],
        out_specs=vmem,
        scratch_shapes=[
            pltpu.VMEM((n * per, rows, LANES), jnp.bfloat16),
            pltpu.VMEM((n - 1, per, rows, LANES), jnp.bfloat16),
            pltpu.VMEM((n * per, rows, LANES), jnp.bfloat16),
            dma,
            dma,
            dma,
            dma,
        ],
        compiler_params=pltpu.CompilerParams(
            collective_id=ident, has_side_effects=True, vmem_limit_bytes=16 * 2**20
        ),
    )(x)


def peak_kernel(n, x_ref, o_ref, landed, send_sem, recv_sem):
    me = lax.axis_index("seq")
    barrier = greet(n, me)
    pl.semaphore_wait(barrier, n - 1)
    out = []
    for off in range(1, n):
        out.append(remote(n, me, off, x_ref, landed.at[off - 1], send_sem, recv_sem))
        out[-1].start()
    top = x_ref[...]
    for off in range(1, n):
        out[off - 1].wait_recv()
        top = jnp.maximum(top, landed[off - 1])
    o_ref[...] = top
    for copy in out:
        copy.wait_send()


def peak_over(x, n, ident):
    tile = 8 * LANES
    padded = -(-x.size // tile) * tile
    flat = jnp.pad(x.reshape(-1), (0, padded - x.size)).reshape(-1, LANES)
    vmem = pl.BlockSpec(memory_space=pltpu.VMEM)
    dma = pltpu.SemaphoreType.DMA((n - 1,))
    top = pl.pallas_call(
        functools.partial(peak_kernel, n),
        out_shape=jax.ShapeDtypeStruct(flat.shape, jnp.float32),
        in_specs=[vmem],
        out_specs=vmem,
        scratch_shapes=[pltpu.VMEM((n - 1,) + flat.shape, jnp.float32), dma, dma],
        compiler_params=pltpu.CompilerParams(
            collective_id=ident, has_side_effects=True, vmem_limit_bytes=16 * 2**20
        ),
    )(flat)
    return top.reshape(-1)[: x.size].reshape(x.shape)


def attend(query, keys, values, new_keys, new_values, live, first, shards, ident):
    batch, steps, heads, group, width = query.shape
    count = keys.shape[1]
    scale = width ** (-0.5)
    key_four = keys.reshape(batch, count, heads, width)
    value_four = values.reshape(batch, count, heads, width)
    cached = (
        jnp.einsum("bskgd,btkd->bksgt", query, key_four, preferred_element_type=jnp.float32) * scale
    )
    fresh = (
        jnp.einsum("bskgd,bukd->bksgu", query, new_keys, preferred_element_type=jnp.float32) * scale
    )
    order = jnp.arange(steps)
    live_mask = live[:, None, None, None, :]
    fresh_mask = ((order[None, :] <= order[:, None]) & first)[None, None, :, None, :]
    cached = jnp.where(live_mask, cached, NEGATIVE)
    fresh = jnp.where(fresh_mask, fresh, NEGATIVE)
    peak = peak_over(jnp.maximum(cached.max(-1), fresh.max(-1)), shards, ident)
    weight_cached = jnp.where(live_mask, jnp.exp(cached - peak[..., None]), 0.0)
    weight_fresh = jnp.where(fresh_mask, jnp.exp(fresh - peak[..., None]), 0.0)
    total = weight_cached.sum(-1) + weight_fresh.sum(-1)
    summed = jnp.einsum(
        "bksgt,btkd->bksgd",
        weight_cached.astype(jnp.bfloat16),
        value_four,
        preferred_element_type=jnp.float32,
    ) + jnp.einsum(
        "bksgu,bukd->bksgd",
        weight_fresh.astype(jnp.bfloat16),
        new_values,
        preferred_element_type=jnp.float32,
    )
    rows, count = steps * batch, heads * group
    totals = total.transpose(2, 0, 1, 3).reshape(rows, count)
    totals = jnp.pad(totals, ((0, 0), (0, -count % LANES)))
    values = summed.transpose(2, 0, 1, 3, 4).reshape(rows, count * width)
    both = sum_over(jnp.concatenate([values, totals], axis=1), shards, ident + 1)
    out = both[:, : count * width].reshape(rows, count, width)
    total = both[:, count * width : count * width + count]
    return (out / total[:, :, None]).astype(jnp.bfloat16).reshape(rows, count * width)


def body(
    thinker_input,
    thinker_gain,
    thinker_qkv,
    thinker_out,
    talker_proj,
    code_table,
    talker_gain,
    talker_qkv,
    talker_out,
    text_keys,
    text_values,
    audio_keys,
    audio_values,
    text_len,
    audio_len,
    text_pos,
    audio_pos,
    code_ids,
):
    steps, batch = thinker_input.shape[:2]
    rows = steps * batch
    index = lax.axis_index("seq")
    shards = lax.axis_size("seq")
    text_kv = HK * HD
    audio_q = AHQ * AHD
    audio_kv = AHK * AHD

    def live_of(cache, lengths):
        count = cache.shape[1]
        return (index * count + jnp.arange(count))[None, :] < lengths[:, None]

    def by_batch(heads):
        return heads.reshape((steps, batch) + heads.shape[1:]).swapaxes(0, 1)

    table_rows = code_table.shape[0]
    table_ids = index * table_rows + jnp.arange(table_rows)
    talker_cols = talker_out.shape[1] // shards
    out_slice = lax.dynamic_slice_in_dim(talker_out, index * talker_cols, talker_cols, 1)
    text_at = text_pos.T.reshape(rows)
    audio_at = audio_pos.T.reshape(rows)
    ids = code_ids.T.reshape(rows)

    inputs = thinker_input.reshape(rows, D).astype(jnp.float32)
    scaled = (inputs * thinker_gain).astype(jnp.bfloat16)
    n = thinker_qkv.shape[0]
    mine = lax.dynamic_slice_in_dim(scaled, index * n, n, 1)
    projected = sum_over(
        jnp.dot(mine, thinker_qkv, preferred_element_type=jnp.float32), shards, 0
    )
    projected = projected * lax.rsqrt(jnp.sum(inputs * inputs, axis=-1) / D + EPSILON)[:, None]
    query = rotate(projected[:, :D].reshape(rows, HQ, HD), text_at).astype(jnp.bfloat16)
    key = rotate(projected[:, D : D + text_kv].reshape(rows, HK, HD), text_at).astype(jnp.bfloat16)
    value = projected[:, D + text_kv :].reshape(rows, HK, HD).astype(jnp.bfloat16)
    attended = attend(
        by_batch(query.reshape(rows, HK, HQ // HK, HD)),
        text_keys,
        text_values,
        by_batch(key),
        by_batch(value),
        live_of(text_keys, text_len),
        index == 0,
        shards,
        1,
    )
    n = thinker_out.shape[0]
    mine = lax.dynamic_slice_in_dim(attended, index * n, n, 1)
    contribution = sum_over(
        jnp.dot(mine, thinker_out, preferred_element_type=jnp.float32), shards, 3
    )
    hidden = (inputs + contribution).astype(jnp.bfloat16)
    picked = (ids[:, None] == table_ids[None, :]).astype(jnp.bfloat16)
    n = talker_proj.shape[0]
    mine = lax.dynamic_slice_in_dim(hidden, index * n, n, 1)
    talker_in = sum_over(
        jnp.dot(mine, talker_proj, preferred_element_type=jnp.float32)
        + jnp.dot(picked, code_table, preferred_element_type=jnp.float32),
        shards,
        4,
    )
    normed = (
        talker_in
        * lax.rsqrt(jnp.sum(talker_in * talker_in, axis=-1, keepdims=True) / TD + EPSILON)
        * talker_gain
    ).astype(jnp.bfloat16)
    spoken = jnp.dot(normed, talker_qkv, preferred_element_type=jnp.float32)
    query = rotate(spoken[:, :audio_q].reshape(rows, AHQ, AHD), audio_at).astype(jnp.bfloat16)
    key = rotate(
        spoken[:, audio_q : audio_q + audio_kv].reshape(rows, AHK, AHD), audio_at
    ).astype(jnp.bfloat16)
    value = spoken[:, audio_q + audio_kv :].reshape(rows, AHK, AHD).astype(jnp.bfloat16)
    heard = attend(
        by_batch(query.reshape(rows, AHK, AHQ // AHK, AHD)),
        audio_keys,
        audio_values,
        by_batch(key),
        by_batch(value),
        live_of(audio_keys, audio_len),
        index == 0,
        shards,
        5,
    )
    residual = lax.dynamic_slice_in_dim(talker_in, index * talker_cols, talker_cols, 1)
    spoken_out = residual + jnp.dot(heard, out_slice, preferred_element_type=jnp.float32)
    return (
        hidden.reshape(steps, batch, D),
        spoken_out.astype(jnp.bfloat16).reshape(steps, batch, talker_cols),
    )


def solution(mesh):
    return jax.shard_map(
        body,
        mesh=mesh,
        in_specs=(
            P(None, "grp", None),
            P(),
            P("seq", None),
            P("seq", None),
            P("seq", None),
            P("seq", None),
            P(),
            P(),
            P(),
            P("grp", "seq", None),
            P("grp", "seq", None),
            P("grp", "seq", None),
            P("grp", "seq", None),
            P("grp"),
            P("grp"),
            P("grp", None),
            P("grp", None),
            P("grp", None),
        ),
        out_specs=(P(None, "grp", None), P(None, "grp", "seq")),
        check_vma=False,
    )
```

```python
import functools

import jax
import jax.numpy as jnp
from jax import lax
from jax.experimental import pallas as pl
from jax.experimental.pallas import tpu as pltpu
from jax.sharding import PartitionSpec as P

D = 3584
HQ = 28
HK = 4
HD = 128
TD = 896
AHQ = 12
AHK = 4
AHD = 128


EPSILON = 1e-06
THETA = 1000000.0
NEGATIVE = -1e30


def rotate(vectors, positions):
    width = vectors.shape[-1]
    half = width // 2
    freqs = jnp.exp(
        jnp.arange(half).astype(jnp.float32) * (-2.0 * jnp.log(jnp.float32(THETA)) / width)
    )
    angles = positions.astype(jnp.float32)[:, None] * freqs[None, :]
    cosine = jnp.cos(angles)[:, None, :]
    sine = jnp.sin(angles)[:, None, :]
    first = vectors[..., :half]
    second = vectors[..., half:]
    return jnp.concatenate(
        [first * cosine - second * sine, second * cosine + first * sine], axis=-1
    )


LANES = 128


def greet(n, me):
    barrier = pltpu.get_barrier_semaphore()
    for off in range(1, n):
        pl.semaphore_signal(
            barrier,
            inc=1,
            device_id={"seq": lax.rem(me + off, n)},
            device_id_type=pl.DeviceIdType.MESH,
        )
    return barrier


def remote(n, me, off, src, dst, send_sem, recv_sem):
    return pltpu.make_async_remote_copy(
        src_ref=src,
        dst_ref=dst,
        send_sem=send_sem.at[off - 1],
        recv_sem=recv_sem.at[off - 1],
        device_id={"seq": lax.rem(me + off, n)},
        device_id_type=pl.DeviceIdType.MESH,
    )


def sum_kernel(n, per, x_ref, o_ref, sent, landed, whole, send_one, recv_one, send_two, recv_two):
    me = lax.axis_index("seq")
    barrier = greet(n, me)
    blocks = x_ref.shape[1] // LANES
    for j in range(blocks):
        sent[j] = x_ref[:, j * LANES : (j + 1) * LANES].astype(sent.dtype)
    for j in range(blocks, n * per):
        sent[j] = jnp.zeros(sent.shape[1:], sent.dtype)
    pl.semaphore_wait(barrier, n - 1)
    out = []
    for off in range(1, n):
        part = pl.ds(lax.rem(me + off, n) * per, per)
        out.append(remote(n, me, off, sent.at[part], landed.at[off - 1], send_one, recv_one))
        out[-1].start()
    mine = pl.ds(me * per, per)
    total = sent[mine].astype(jnp.float32)
    for off in range(1, n):
        out[off - 1].wait_recv()
        total = total + landed[off - 1].astype(jnp.float32)
    whole[mine] = total.astype(whole.dtype)
    back = []
    for off in range(1, n):
        back.append(remote(n, me, off, whole.at[mine], whole.at[mine], send_two, recv_two))
        back[-1].start()
    for copy in out:
        copy.wait_send()
    for copy in back:
        copy.wait_recv()
    for j in range(blocks):
        o_ref[:, j * LANES : (j + 1) * LANES] = whole[j].astype(o_ref.dtype)
    for copy in back:
        copy.wait_send()


def sum_over(x, n, ident):
    rows, columns = x.shape
    per = -(-(columns // LANES) // n)
    vmem = pl.BlockSpec(memory_space=pltpu.VMEM)
    dma = pltpu.SemaphoreType.DMA((n - 1,))
    return pl.pallas_call(
        functools.partial(sum_kernel, n, per),
        out_shape=jax.ShapeDtypeStruct(x.shape, jnp.float32),
        in_specs=[vmem],
        out_specs=vmem,
        scratch_shapes=[
            pltpu.VMEM((n * per, rows, LANES), jnp.bfloat16),
            pltpu.VMEM((n - 1, per, rows, LANES), jnp.bfloat16),
            pltpu.VMEM((n * per, rows, LANES), jnp.bfloat16),
            dma,
            dma,
            dma,
            dma,
        ],
        compiler_params=pltpu.CompilerParams(
            collective_id=ident, has_side_effects=True, vmem_limit_bytes=16 * 2**20
        ),
    )(x)


def merge_kernel(
    n, per, x_ref, lse_ref, o_ref, sent, landed, logs, whole, send_one, recv_one, send_log, recv_log, send_two, recv_two
):
    me = lax.axis_index("seq")
    barrier = greet(n, me)
    blocks = x_ref.shape[1] // LANES
    for j in range(blocks):
        sent[j] = x_ref[:, j * LANES : (j + 1) * LANES]
    for j in range(blocks, n * per):
        sent[j] = jnp.zeros(sent.shape[1:], sent.dtype)
    pl.semaphore_wait(barrier, n - 1)
    out, told = [], []
    for off in range(1, n):
        told.append(remote(n, me, off, lse_ref, logs.at[off - 1], send_log, recv_log))
        told[-1].start()
        part = pl.ds(lax.rem(me + off, n) * per, per)
        out.append(remote(n, me, off, sent.at[part], landed.at[off - 1], send_one, recv_one))
        out[-1].start()
    for copy in told:
        copy.wait_recv()
    lse = [lse_ref[...]] + [logs[off - 1] for off in range(1, n)]
    top = functools.reduce(jnp.maximum, lse)
    weights = [jnp.exp(one - top) for one in lse]
    scale = 1.0 / functools.reduce(jnp.add, weights)
    lane = lax.broadcasted_iota(jnp.int32, top.shape, 1)

    def column(weight, p):
        here = lane == me * per + p
        return jnp.sum(jnp.where(here, weight * scale, 0.0), axis=1, keepdims=True)

    total = [column(weights[0], p) * sent[me * per + p].astype(jnp.float32) for p in range(per)]
    for off in range(1, n):
        out[off - 1].wait_recv()
        for p in range(per):
            total[p] = total[p] + column(weights[off], p) * landed[off - 1, p].astype(jnp.float32)
    for p in range(per):
        whole[me * per + p] = total[p].astype(whole.dtype)
    mine = pl.ds(me * per, per)
    back = []
    for off in range(1, n):
        back.append(remote(n, me, off, whole.at[mine], whole.at[mine], send_two, recv_two))
        back[-1].start()
    for copy in told + out:
        copy.wait_send()
    for copy in back:
        copy.wait_recv()
    for j in range(blocks):
        o_ref[:, j * LANES : (j + 1) * LANES] = whole[j]
    for copy in back:
        copy.wait_send()


def merge_over(values, lse, n, ident):
    rows, columns = values.shape
    per = -(-(columns // LANES) // n)
    vmem = pl.BlockSpec(memory_space=pltpu.VMEM)
    dma = pltpu.SemaphoreType.DMA((n - 1,))
    return pl.pallas_call(
        functools.partial(merge_kernel, n, per),
        out_shape=jax.ShapeDtypeStruct(values.shape, jnp.bfloat16),
        in_specs=[vmem, vmem],
        out_specs=vmem,
        scratch_shapes=[
            pltpu.VMEM((n * per, rows, LANES), jnp.bfloat16),
            pltpu.VMEM((n - 1, per, rows, LANES), jnp.bfloat16),
            pltpu.VMEM((n - 1, rows, LANES), jnp.float32),
            pltpu.VMEM((n * per, rows, LANES), jnp.bfloat16),
        ]
        + [dma] * 6,
        compiler_params=pltpu.CompilerParams(
            collective_id=ident, has_side_effects=True, vmem_limit_bytes=16 * 2**20
        ),
    )(values, lse)


def attend_kernel(steps, group, len_ref, q_ref, k_ref, v_ref, nk_ref, nv_ref, o_ref, lse_ref):
    me = lax.axis_index("seq")
    heads, padded, width = q_ref.shape[1:]
    count = k_ref.shape[1]
    fresh_count = nk_ref.shape[2]
    scale = width ** (-0.5)
    length = len_ref[pl.program_id(0)]
    place = me * count + lax.broadcasted_iota(jnp.int32, (padded, count), 1)
    live = place < length
    row = lax.broadcasted_iota(jnp.int32, (padded, fresh_count), 0)
    slot = lax.broadcasted_iota(jnp.int32, (padded, fresh_count), 1)
    fresh_live = (slot * group <= row) & (slot < steps) & (me == 0)
    across = (((1,), (1,)), ((), ()))
    for k in range(heads):
        part = slice(k * width, (k + 1) * width)
        q = q_ref[0, k]
        cached = lax.dot_general(q, k_ref[0, :, part], across, preferred_element_type=jnp.float32)
        fresh = lax.dot_general(q, nk_ref[0, k], across, preferred_element_type=jnp.float32)
        cached = jnp.where(live, cached * scale, NEGATIVE)
        fresh = jnp.where(fresh_live, fresh * scale, NEGATIVE)
        peak = jnp.maximum(
            jnp.max(cached, axis=1, keepdims=True), jnp.max(fresh, axis=1, keepdims=True)
        )
        weight = jnp.where(live, jnp.exp(cached - peak), 0.0)
        weight_fresh = jnp.where(fresh_live, jnp.exp(fresh - peak), 0.0)
        total = jnp.sum(weight, axis=1, keepdims=True) + jnp.sum(
            weight_fresh, axis=1, keepdims=True
        )
        summed = jnp.dot(
            weight.astype(jnp.bfloat16), v_ref[0, :, part], preferred_element_type=jnp.float32
        ) + jnp.dot(
            weight_fresh.astype(jnp.bfloat16), nv_ref[0, k], preferred_element_type=jnp.float32
        )
        safe = jnp.maximum(total, 0.5)
        o_ref[0, k] = (summed / safe).astype(o_ref.dtype)
        log = jnp.where(total > 0.5, peak + jnp.log(safe), NEGATIVE)
        lse_ref[0, k] = jnp.broadcast_to(log, (padded, width))


def attend(query, keys, values, new_keys, new_values, lengths, shards, ident):
    batch, steps, heads, group, width = query.shape
    count = keys.shape[1]
    used = steps * group
    padded = -(-used // 16) * 16
    quest = query.transpose(0, 2, 1, 3, 4).reshape(batch, heads, used, width)
    quest = jnp.pad(quest, ((0, 0), (0, 0), (0, padded - used), (0, 0)))

    def slots(new):
        return jnp.pad(new.transpose(0, 2, 1, 3), ((0, 0), (0, 0), (0, -steps % 16), (0, 0)))

    new_keys, new_values = slots(new_keys), slots(new_values)

    def spec(shape):
        return pl.BlockSpec((1,) + shape, lambda b: (b,) + (0,) * len(shape))

    cache = spec((count, heads * width))
    fresh = spec(new_keys.shape[1:])
    rows_spec = spec((heads, padded, width))
    out, lse = pl.pallas_call(
        functools.partial(attend_kernel, steps, group),
        grid=(batch,),
        out_shape=(
            jax.ShapeDtypeStruct(quest.shape, jnp.bfloat16),
            jax.ShapeDtypeStruct(quest.shape, jnp.float32),
        ),
        in_specs=[
            pl.BlockSpec(memory_space=pltpu.SMEM), rows_spec, cache, cache, fresh, fresh
        ],
        out_specs=(rows_spec, rows_spec),
        compiler_params=pltpu.CompilerParams(vmem_limit_bytes=16 * 2**20),
    )(lengths, quest, keys, values, new_keys, new_values)

    def by_row(x):
        x = x[:, :, :used].reshape(batch, heads, steps, group, -1).transpose(2, 0, 1, 3, 4)
        return x.reshape(steps * batch, -1)

    logs = by_row(lse[..., :1])
    logs = jnp.pad(logs, ((0, 0), (0, LANES - logs.shape[1])))
    return merge_over(by_row(out), logs, shards, ident)


def body(
    thinker_input,
    thinker_gain,
    thinker_qkv,
    thinker_out,
    talker_proj,
    code_table,
    talker_gain,
    talker_qkv,
    talker_out,
    text_keys,
    text_values,
    audio_keys,
    audio_values,
    text_len,
    audio_len,
    text_pos,
    audio_pos,
    code_ids,
):
    steps, batch = thinker_input.shape[:2]
    rows = steps * batch
    index = lax.axis_index("seq")
    shards = lax.axis_size("seq")
    text_kv = HK * HD
    audio_q = AHQ * AHD
    audio_kv = AHK * AHD

    def by_batch(heads):
        return heads.reshape((steps, batch) + heads.shape[1:]).swapaxes(0, 1)

    table_rows = code_table.shape[0]
    table_ids = index * table_rows + jnp.arange(table_rows)
    talker_cols = talker_out.shape[1] // shards
    out_slice = lax.dynamic_slice_in_dim(talker_out, index * talker_cols, talker_cols, 1)
    text_at = text_pos.T.reshape(rows)
    audio_at = audio_pos.T.reshape(rows)
    ids = code_ids.T.reshape(rows)

    inputs = thinker_input.reshape(rows, D).astype(jnp.float32)
    scaled = (inputs * thinker_gain).astype(jnp.bfloat16)
    n = thinker_qkv.shape[0]
    mine = lax.dynamic_slice_in_dim(scaled, index * n, n, 1)
    projected = sum_over(
        jnp.dot(mine, thinker_qkv, preferred_element_type=jnp.float32), shards, 0
    )
    projected = projected * lax.rsqrt(jnp.sum(inputs * inputs, axis=-1) / D + EPSILON)[:, None]
    query = rotate(projected[:, :D].reshape(rows, HQ, HD), text_at).astype(jnp.bfloat16)
    key = rotate(projected[:, D : D + text_kv].reshape(rows, HK, HD), text_at).astype(jnp.bfloat16)
    value = projected[:, D + text_kv :].reshape(rows, HK, HD).astype(jnp.bfloat16)
    attended = attend(
        by_batch(query.reshape(rows, HK, HQ // HK, HD)),
        text_keys,
        text_values,
        by_batch(key),
        by_batch(value),
        text_len,
        shards,
        1,
    )
    n = thinker_out.shape[0]
    mine = lax.dynamic_slice_in_dim(attended, index * n, n, 1)
    contribution = sum_over(
        jnp.dot(mine, thinker_out, preferred_element_type=jnp.float32), shards, 3
    )
    hidden = (inputs + contribution).astype(jnp.bfloat16)
    picked = (ids[:, None] == table_ids[None, :]).astype(jnp.bfloat16)
    n = talker_proj.shape[0]
    mine = lax.dynamic_slice_in_dim(hidden, index * n, n, 1)
    talker_in = sum_over(
        jnp.dot(mine, talker_proj, preferred_element_type=jnp.float32)
        + jnp.dot(picked, code_table, preferred_element_type=jnp.float32),
        shards,
        4,
    )
    normed = (
        talker_in
        * lax.rsqrt(jnp.sum(talker_in * talker_in, axis=-1, keepdims=True) / TD + EPSILON)
        * talker_gain
    ).astype(jnp.bfloat16)
    spoken = jnp.dot(normed, talker_qkv, preferred_element_type=jnp.float32)
    query = rotate(spoken[:, :audio_q].reshape(rows, AHQ, AHD), audio_at).astype(jnp.bfloat16)
    key = rotate(
        spoken[:, audio_q : audio_q + audio_kv].reshape(rows, AHK, AHD), audio_at
    ).astype(jnp.bfloat16)
    value = spoken[:, audio_q + audio_kv :].reshape(rows, AHK, AHD).astype(jnp.bfloat16)
    heard = attend(
        by_batch(query.reshape(rows, AHK, AHQ // AHK, AHD)),
        audio_keys,
        audio_values,
        by_batch(key),
        by_batch(value),
        audio_len,
        shards,
        5,
    )
    residual = lax.dynamic_slice_in_dim(talker_in, index * talker_cols, talker_cols, 1)
    spoken_out = residual + jnp.dot(heard, out_slice, preferred_element_type=jnp.float32)
    return (
        hidden.reshape(steps, batch, D),
        spoken_out.astype(jnp.bfloat16).reshape(steps, batch, talker_cols),
    )


def solution(mesh):
    return jax.shard_map(
        body,
        mesh=mesh,
        in_specs=(
            P(None, "grp", None),
            P(),
            P("seq", None),
            P("seq", None),
            P("seq", None),
            P("seq", None),
            P(),
            P(),
            P(),
            P("grp", "seq", None),
            P("grp", "seq", None),
            P("grp", "seq", None),
            P("grp", "seq", None),
            P("grp"),
            P("grp"),
            P("grp", None),
            P("grp", None),
            P("grp", None),
        ),
        out_specs=(P(None, "grp", None), P(None, "grp", "seq")),
        check_vma=False,
    )
```

```python
import functools
import math

import jax
import jax.numpy as jnp
from jax import lax
from jax.experimental import pallas as pl
from jax.experimental.pallas import tpu as pltpu
from jax.sharding import PartitionSpec as P

D = 3584
HQ = 28
HK = 4
HD = 128
TD = 896
AHQ = 12
AHK = 4
AHD = 128


EPSILON = 1e-06
THETA = 1000000.0
NEGATIVE = -1e30


def rotate(vectors, positions):
    width = vectors.shape[-1]
    half = width // 2
    freqs = jnp.exp(
        jnp.arange(half).astype(jnp.float32) * (-2.0 * jnp.log(jnp.float32(THETA)) / width)
    )
    angles = positions.astype(jnp.float32)[:, None] * freqs[None, :]
    cosine = jnp.cos(angles)[:, None, :]
    sine = jnp.sin(angles)[:, None, :]
    first = vectors[..., :half]
    second = vectors[..., half:]
    return jnp.concatenate(
        [first * cosine - second * sine, second * cosine + first * sine], axis=-1
    )


LANES = 128


def greet(n, me):
    barrier = pltpu.get_barrier_semaphore()
    for off in range(1, n):
        pl.semaphore_signal(
            barrier,
            inc=1,
            device_id={"seq": lax.rem(me + off, n)},
            device_id_type=pl.DeviceIdType.MESH,
        )
    return barrier


def remote(n, me, off, src, dst, send_sem, recv_sem):
    return pltpu.make_async_remote_copy(
        src_ref=src,
        dst_ref=dst,
        send_sem=send_sem.at[off - 1],
        recv_sem=recv_sem.at[off - 1],
        device_id={"seq": lax.rem(me + off, n)},
        device_id_type=pl.DeviceIdType.MESH,
    )


def sum_kernel(n, per, x_ref, o_ref, sent, landed, whole, send_one, recv_one, send_two, recv_two):
    me = lax.axis_index("seq")
    barrier = greet(n, me)
    blocks = x_ref.shape[1] // LANES
    for j in range(blocks):
        sent[j] = x_ref[:, j * LANES : (j + 1) * LANES].astype(sent.dtype)
    for j in range(blocks, n * per):
        sent[j] = jnp.zeros(sent.shape[1:], sent.dtype)
    pl.semaphore_wait(barrier, n - 1)
    out = []
    for off in range(1, n):
        part = pl.ds(lax.rem(me + off, n) * per, per)
        out.append(remote(n, me, off, sent.at[part], landed.at[off - 1], send_one, recv_one))
        out[-1].start()
    mine = pl.ds(me * per, per)
    total = sent[mine].astype(jnp.float32)
    for off in range(1, n):
        out[off - 1].wait_recv()
        total = total + landed[off - 1].astype(jnp.float32)
    whole[mine] = total.astype(whole.dtype)
    back = []
    for off in range(1, n):
        back.append(remote(n, me, off, whole.at[mine], whole.at[mine], send_two, recv_two))
        back[-1].start()
    for copy in out:
        copy.wait_send()
    for copy in back:
        copy.wait_recv()
    for j in range(blocks):
        o_ref[:, j * LANES : (j + 1) * LANES] = whole[j].astype(o_ref.dtype)
    for copy in back:
        copy.wait_send()


def sum_over(x, n, ident):
    rows, columns = x.shape
    per = -(-(columns // LANES) // n)
    vmem = pl.BlockSpec(memory_space=pltpu.VMEM)
    dma = pltpu.SemaphoreType.DMA((n - 1,))
    return pl.pallas_call(
        functools.partial(sum_kernel, n, per),
        out_shape=jax.ShapeDtypeStruct(x.shape, jnp.float32),
        in_specs=[vmem],
        out_specs=vmem,
        scratch_shapes=[
            pltpu.VMEM((n * per, rows, LANES), jnp.bfloat16),
            pltpu.VMEM((n - 1, per, rows, LANES), jnp.bfloat16),
            pltpu.VMEM((n * per, rows, LANES), jnp.bfloat16),
            dma,
            dma,
            dma,
            dma,
        ],
        compiler_params=pltpu.CompilerParams(
            collective_id=ident, has_side_effects=True, vmem_limit_bytes=16 * 2**20
        ),
    )(x)


def merge_kernel(
    n, per, x_ref, lse_ref, o_ref, sent, landed, logs, whole, send_one, recv_one, send_log, recv_log, send_two, recv_two
):
    me = lax.axis_index("seq")
    barrier = greet(n, me)
    blocks = x_ref.shape[1] // LANES
    for j in range(blocks):
        sent[j] = x_ref[:, j * LANES : (j + 1) * LANES]
    for j in range(blocks, n * per):
        sent[j] = jnp.zeros(sent.shape[1:], sent.dtype)
    pl.semaphore_wait(barrier, n - 1)
    out, told = [], []
    for off in range(1, n):
        told.append(remote(n, me, off, lse_ref, logs.at[off - 1], send_log, recv_log))
        told[-1].start()
        part = pl.ds(lax.rem(me + off, n) * per, per)
        out.append(remote(n, me, off, sent.at[part], landed.at[off - 1], send_one, recv_one))
        out[-1].start()
    for copy in told:
        copy.wait_recv()
    lse = [lse_ref[...]] + [logs[off - 1] for off in range(1, n)]
    top = functools.reduce(jnp.maximum, lse)
    weights = [jnp.exp(one - top) for one in lse]
    scale = 1.0 / functools.reduce(jnp.add, weights)
    lane = lax.broadcasted_iota(jnp.int32, top.shape, 1)

    def column(weight, p):
        here = lane == me * per + p
        return jnp.sum(jnp.where(here, weight * scale, 0.0), axis=1, keepdims=True)

    total = [column(weights[0], p) * sent[me * per + p].astype(jnp.float32) for p in range(per)]
    for off in range(1, n):
        out[off - 1].wait_recv()
        for p in range(per):
            total[p] = total[p] + column(weights[off], p) * landed[off - 1, p].astype(jnp.float32)
    for p in range(per):
        whole[me * per + p] = total[p].astype(whole.dtype)
    mine = pl.ds(me * per, per)
    back = []
    for off in range(1, n):
        back.append(remote(n, me, off, whole.at[mine], whole.at[mine], send_two, recv_two))
        back[-1].start()
    for copy in told + out:
        copy.wait_send()
    for copy in back:
        copy.wait_recv()
    for j in range(blocks):
        o_ref[:, j * LANES : (j + 1) * LANES] = whole[j]
    for copy in back:
        copy.wait_send()


def merge_over(values, lse, n, ident):
    rows, columns = values.shape
    per = -(-(columns // LANES) // n)
    vmem = pl.BlockSpec(memory_space=pltpu.VMEM)
    dma = pltpu.SemaphoreType.DMA((n - 1,))
    return pl.pallas_call(
        functools.partial(merge_kernel, n, per),
        out_shape=jax.ShapeDtypeStruct(values.shape, jnp.bfloat16),
        in_specs=[vmem, vmem],
        out_specs=vmem,
        scratch_shapes=[
            pltpu.VMEM((n * per, rows, LANES), jnp.bfloat16),
            pltpu.VMEM((n - 1, per, rows, LANES), jnp.bfloat16),
            pltpu.VMEM((n - 1, rows, LANES), jnp.float32),
            pltpu.VMEM((n * per, rows, LANES), jnp.bfloat16),
        ]
        + [dma] * 6,
        compiler_params=pltpu.CompilerParams(
            collective_id=ident, has_side_effects=True, vmem_limit_bytes=16 * 2**20
        ),
    )(values, lse)


def attend_kernel(steps, group, len_ref, q_ref, k_ref, v_ref, nk_ref, nv_ref, o_ref, lse_ref):
    me = lax.axis_index("seq")
    heads, padded, width = q_ref.shape[1:]
    count = k_ref.shape[1]
    fresh_count = nk_ref.shape[2]
    scale = width ** (-0.5)
    fold = q_ref.shape[0]
    place = me * count + lax.broadcasted_iota(jnp.int32, (padded, count), 1)
    row = lax.broadcasted_iota(jnp.int32, (padded, fresh_count), 0)
    slot = lax.broadcasted_iota(jnp.int32, (padded, fresh_count), 1)
    fresh_live = (slot * group <= row) & (slot < steps) & (me == 0)
    across = (((1,), (1,)), ((), ()))
    for c, k in [(c, k) for c in range(fold) for k in range(heads)]:
        live = place < len_ref[pl.program_id(0) * fold + c]
        part = slice(k * width, (k + 1) * width)
        q = q_ref[c, k]
        cached = lax.dot_general(q, k_ref[c, :, part], across, preferred_element_type=jnp.float32)
        fresh = lax.dot_general(q, nk_ref[c, k], across, preferred_element_type=jnp.float32)
        cached = jnp.where(live, cached * scale, NEGATIVE)
        fresh = jnp.where(fresh_live, fresh * scale, NEGATIVE)
        peak = jnp.maximum(
            jnp.max(cached, axis=1, keepdims=True), jnp.max(fresh, axis=1, keepdims=True)
        )
        weight = jnp.where(live, jnp.exp(cached - peak), 0.0)
        weight_fresh = jnp.where(fresh_live, jnp.exp(fresh - peak), 0.0)
        total = jnp.sum(weight, axis=1, keepdims=True) + jnp.sum(
            weight_fresh, axis=1, keepdims=True
        )
        summed = jnp.dot(
            weight.astype(jnp.bfloat16), v_ref[c, :, part], preferred_element_type=jnp.float32
        ) + jnp.dot(
            weight_fresh.astype(jnp.bfloat16), nv_ref[c, k], preferred_element_type=jnp.float32
        )
        safe = jnp.maximum(total, 0.5)
        o_ref[c, k] = (summed / safe).astype(o_ref.dtype)
        log = jnp.where(total > 0.5, peak + jnp.log(safe), NEGATIVE)
        lse_ref[c, k] = jnp.broadcast_to(log, (padded, width))


def attend(query, keys, values, new_keys, new_values, lengths, shards, ident):
    batch, steps, heads, group, width = query.shape
    count = keys.shape[1]
    fold = math.gcd(batch, 4)
    used = steps * group
    padded = -(-used // 16) * 16
    quest = query.transpose(0, 2, 1, 3, 4).reshape(batch, heads, used, width)
    quest = jnp.pad(quest, ((0, 0), (0, 0), (0, padded - used), (0, 0)))

    def slots(new):
        return jnp.pad(new.transpose(0, 2, 1, 3), ((0, 0), (0, 0), (0, -steps % 16), (0, 0)))

    new_keys, new_values = slots(new_keys), slots(new_values)

    def spec(shape):
        return pl.BlockSpec((fold,) + shape, lambda b: (b,) + (0,) * len(shape))

    cache = spec((count, heads * width))
    fresh = spec(new_keys.shape[1:])
    rows_spec = spec((heads, padded, width))
    out, lse = pl.pallas_call(
        functools.partial(attend_kernel, steps, group),
        grid=(batch // fold,),
        out_shape=(
            jax.ShapeDtypeStruct(quest.shape, jnp.bfloat16),
            jax.ShapeDtypeStruct(quest.shape, jnp.float32),
        ),
        in_specs=[
            pl.BlockSpec(memory_space=pltpu.SMEM), rows_spec, cache, cache, fresh, fresh
        ],
        out_specs=(rows_spec, rows_spec),
        compiler_params=pltpu.CompilerParams(vmem_limit_bytes=16 * 2**20),
    )(lengths, quest, keys, values, new_keys, new_values)

    def by_row(x):
        x = x[:, :, :used].reshape(batch, heads, steps, group, -1).transpose(2, 0, 1, 3, 4)
        return x.reshape(steps * batch, -1)

    logs = by_row(lse[..., :1])
    logs = jnp.pad(logs, ((0, 0), (0, LANES - logs.shape[1])))
    return merge_over(by_row(out), logs, shards, ident)


def body(
    thinker_input,
    thinker_gain,
    thinker_qkv,
    thinker_out,
    talker_proj,
    code_table,
    talker_gain,
    talker_qkv,
    talker_out,
    text_keys,
    text_values,
    audio_keys,
    audio_values,
    text_len,
    audio_len,
    text_pos,
    audio_pos,
    code_ids,
):
    steps, batch = thinker_input.shape[:2]
    rows = steps * batch
    index = lax.axis_index("seq")
    shards = lax.axis_size("seq")
    text_kv = HK * HD
    audio_q = AHQ * AHD
    audio_kv = AHK * AHD

    def by_batch(heads):
        return heads.reshape((steps, batch) + heads.shape[1:]).swapaxes(0, 1)

    table_rows = code_table.shape[0]
    table_ids = index * table_rows + jnp.arange(table_rows)
    talker_cols = talker_out.shape[1] // shards
    out_slice = lax.dynamic_slice_in_dim(talker_out, index * talker_cols, talker_cols, 1)
    text_at = text_pos.T.reshape(rows)
    audio_at = audio_pos.T.reshape(rows)
    ids = code_ids.T.reshape(rows)

    inputs = thinker_input.reshape(rows, D).astype(jnp.float32)
    scaled = (inputs * thinker_gain).astype(jnp.bfloat16)
    n = thinker_qkv.shape[0]
    mine = lax.dynamic_slice_in_dim(scaled, index * n, n, 1)
    projected = sum_over(
        jnp.dot(mine, thinker_qkv, preferred_element_type=jnp.float32), shards, 0
    )
    projected = projected * lax.rsqrt(jnp.sum(inputs * inputs, axis=-1) / D + EPSILON)[:, None]
    query = rotate(projected[:, :D].reshape(rows, HQ, HD), text_at).astype(jnp.bfloat16)
    key = rotate(projected[:, D : D + text_kv].reshape(rows, HK, HD), text_at).astype(jnp.bfloat16)
    value = projected[:, D + text_kv :].reshape(rows, HK, HD).astype(jnp.bfloat16)
    attended = attend(
        by_batch(query.reshape(rows, HK, HQ // HK, HD)),
        text_keys,
        text_values,
        by_batch(key),
        by_batch(value),
        text_len,
        shards,
        1,
    )
    n = thinker_out.shape[0]
    mine = lax.dynamic_slice_in_dim(attended, index * n, n, 1)
    contribution = sum_over(
        jnp.dot(mine, thinker_out, preferred_element_type=jnp.float32), shards, 3
    )
    hidden = (inputs + contribution).astype(jnp.bfloat16)
    picked = (ids[:, None] == table_ids[None, :]).astype(jnp.bfloat16)
    n = talker_proj.shape[0]
    mine = lax.dynamic_slice_in_dim(hidden, index * n, n, 1)
    talker_in = sum_over(
        jnp.dot(mine, talker_proj, preferred_element_type=jnp.float32)
        + jnp.dot(picked, code_table, preferred_element_type=jnp.float32),
        shards,
        4,
    )
    normed = (
        talker_in
        * lax.rsqrt(jnp.sum(talker_in * talker_in, axis=-1, keepdims=True) / TD + EPSILON)
        * talker_gain
    ).astype(jnp.bfloat16)
    spoken = jnp.dot(normed, talker_qkv, preferred_element_type=jnp.float32)
    query = rotate(spoken[:, :audio_q].reshape(rows, AHQ, AHD), audio_at).astype(jnp.bfloat16)
    key = rotate(
        spoken[:, audio_q : audio_q + audio_kv].reshape(rows, AHK, AHD), audio_at
    ).astype(jnp.bfloat16)
    value = spoken[:, audio_q + audio_kv :].reshape(rows, AHK, AHD).astype(jnp.bfloat16)
    heard = attend(
        by_batch(query.reshape(rows, AHK, AHQ // AHK, AHD)),
        audio_keys,
        audio_values,
        by_batch(key),
        by_batch(value),
        audio_len,
        shards,
        5,
    )
    residual = lax.dynamic_slice_in_dim(talker_in, index * talker_cols, talker_cols, 1)
    spoken_out = residual + jnp.dot(heard, out_slice, preferred_element_type=jnp.float32)
    return (
        hidden.reshape(steps, batch, D),
        spoken_out.astype(jnp.bfloat16).reshape(steps, batch, talker_cols),
    )


def solution(mesh):
    return jax.shard_map(
        body,
        mesh=mesh,
        in_specs=(
            P(None, "grp", None),
            P(),
            P("seq", None),
            P("seq", None),
            P("seq", None),
            P("seq", None),
            P(),
            P(),
            P(),
            P("grp", "seq", None),
            P("grp", "seq", None),
            P("grp", "seq", None),
            P("grp", "seq", None),
            P("grp"),
            P("grp"),
            P("grp", None),
            P("grp", None),
            P("grp", None),
        ),
        out_specs=(P(None, "grp", None), P(None, "grp", "seq")),
        check_vma=False,
    )
```

```python
import functools
import math

import jax
import jax.numpy as jnp
from jax import lax
from jax.experimental import pallas as pl
from jax.experimental.pallas import tpu as pltpu
from jax.sharding import PartitionSpec as P

D = 3584
HQ = 28
HK = 4
HD = 128
TD = 896
AHQ = 12
AHK = 4
AHD = 128


EPSILON = 1e-06
THETA = 1000000.0
NEGATIVE = -1e30


def rotate(vectors, positions):
    width = vectors.shape[-1]
    half = width // 2
    freqs = jnp.exp(
        jnp.arange(half).astype(jnp.float32) * (-2.0 * jnp.log(jnp.float32(THETA)) / width)
    )
    angles = positions.astype(jnp.float32)[:, None] * freqs[None, :]
    cosine = jnp.cos(angles)[:, None, :]
    sine = jnp.sin(angles)[:, None, :]
    first = vectors[..., :half]
    second = vectors[..., half:]
    return jnp.concatenate(
        [first * cosine - second * sine, second * cosine + first * sine], axis=-1
    )


LANES = 128


def greet(n, me):
    barrier = pltpu.get_barrier_semaphore()
    for off in range(1, n):
        pl.semaphore_signal(
            barrier,
            inc=1,
            device_id={"seq": lax.rem(me + off, n)},
            device_id_type=pl.DeviceIdType.MESH,
        )
    return barrier


def remote(n, me, off, src, dst, send_sem, recv_sem):
    return pltpu.make_async_remote_copy(
        src_ref=src,
        dst_ref=dst,
        send_sem=send_sem.at[off - 1],
        recv_sem=recv_sem.at[off - 1],
        device_id={"seq": lax.rem(me + off, n)},
        device_id_type=pl.DeviceIdType.MESH,
    )


def sum_kernel(n, per, x_ref, o_ref, sent, landed, whole, send_one, recv_one, send_two, recv_two):
    me = lax.axis_index("seq")
    barrier = greet(n, me)
    blocks = x_ref.shape[1] // LANES
    for j in range(blocks):
        sent[j] = x_ref[:, j * LANES : (j + 1) * LANES].astype(sent.dtype)
    for j in range(blocks, n * per):
        sent[j] = jnp.zeros(sent.shape[1:], sent.dtype)
    pl.semaphore_wait(barrier, n - 1)
    out = []
    for off in range(1, n):
        part = pl.ds(lax.rem(me + off, n) * per, per)
        out.append(remote(n, me, off, sent.at[part], landed.at[off - 1], send_one, recv_one))
        out[-1].start()
    mine = pl.ds(me * per, per)
    total = sent[mine].astype(jnp.float32)
    for off in range(1, n):
        out[off - 1].wait_recv()
        total = total + landed[off - 1].astype(jnp.float32)
    whole[mine] = total.astype(whole.dtype)
    back = []
    for off in range(1, n):
        back.append(remote(n, me, off, whole.at[mine], whole.at[mine], send_two, recv_two))
        back[-1].start()
    for copy in out:
        copy.wait_send()
    for copy in back:
        copy.wait_recv()
    for j in range(blocks):
        o_ref[:, j * LANES : (j + 1) * LANES] = whole[j].astype(o_ref.dtype)
    for copy in back:
        copy.wait_send()


def sum_over(x, n, ident):
    rows, columns = x.shape
    per = -(-(columns // LANES) // n)
    vmem = pl.BlockSpec(memory_space=pltpu.VMEM)
    dma = pltpu.SemaphoreType.DMA((n - 1,))
    return pl.pallas_call(
        functools.partial(sum_kernel, n, per),
        out_shape=jax.ShapeDtypeStruct(x.shape, jnp.bfloat16),
        in_specs=[vmem],
        out_specs=vmem,
        scratch_shapes=[
            pltpu.VMEM((n * per, rows, LANES), jnp.bfloat16),
            pltpu.VMEM((n - 1, per, rows, LANES), jnp.bfloat16),
            pltpu.VMEM((n * per, rows, LANES), jnp.bfloat16),
            dma,
            dma,
            dma,
            dma,
        ],
        compiler_params=pltpu.CompilerParams(
            collective_id=ident, has_side_effects=True, vmem_limit_bytes=16 * 2**20
        ),
    )(x.astype(jnp.bfloat16)).astype(jnp.float32)


def merge_kernel(
    n, per, x_ref, lse_ref, o_ref, sent, landed, logs, whole, send_one, recv_one, send_log, recv_log, send_two, recv_two
):
    me = lax.axis_index("seq")
    barrier = greet(n, me)
    blocks = x_ref.shape[1] // LANES
    for j in range(blocks):
        sent[j] = x_ref[:, j * LANES : (j + 1) * LANES]
    for j in range(blocks, n * per):
        sent[j] = jnp.zeros(sent.shape[1:], sent.dtype)
    pl.semaphore_wait(barrier, n - 1)
    out, told = [], []
    for off in range(1, n):
        told.append(remote(n, me, off, lse_ref, logs.at[off - 1], send_log, recv_log))
        told[-1].start()
        part = pl.ds(lax.rem(me + off, n) * per, per)
        out.append(remote(n, me, off, sent.at[part], landed.at[off - 1], send_one, recv_one))
        out[-1].start()
    for copy in told:
        copy.wait_recv()
    lse = [lse_ref[...]] + [logs[off - 1] for off in range(1, n)]
    top = functools.reduce(jnp.maximum, lse)
    weights = [jnp.exp(one - top) for one in lse]
    scale = 1.0 / functools.reduce(jnp.add, weights)
    lane = lax.broadcasted_iota(jnp.int32, top.shape, 1)

    def column(weight, p):
        here = lane == me * per + p
        return jnp.sum(jnp.where(here, weight * scale, 0.0), axis=1, keepdims=True)

    total = [column(weights[0], p) * sent[me * per + p].astype(jnp.float32) for p in range(per)]
    for off in range(1, n):
        out[off - 1].wait_recv()
        for p in range(per):
            total[p] = total[p] + column(weights[off], p) * landed[off - 1, p].astype(jnp.float32)
    for p in range(per):
        whole[me * per + p] = total[p].astype(whole.dtype)
    mine = pl.ds(me * per, per)
    back = []
    for off in range(1, n):
        back.append(remote(n, me, off, whole.at[mine], whole.at[mine], send_two, recv_two))
        back[-1].start()
    for copy in told + out:
        copy.wait_send()
    for copy in back:
        copy.wait_recv()
    for j in range(blocks):
        o_ref[:, j * LANES : (j + 1) * LANES] = whole[j]
    for copy in back:
        copy.wait_send()


def merge_over(values, lse, n, ident):
    rows, columns = values.shape
    per = -(-(columns // LANES) // n)
    vmem = pl.BlockSpec(memory_space=pltpu.VMEM)
    dma = pltpu.SemaphoreType.DMA((n - 1,))
    return pl.pallas_call(
        functools.partial(merge_kernel, n, per),
        out_shape=jax.ShapeDtypeStruct(values.shape, jnp.bfloat16),
        in_specs=[vmem, vmem],
        out_specs=vmem,
        scratch_shapes=[
            pltpu.VMEM((n * per, rows, LANES), jnp.bfloat16),
            pltpu.VMEM((n - 1, per, rows, LANES), jnp.bfloat16),
            pltpu.VMEM((n - 1, rows, LANES), jnp.float32),
            pltpu.VMEM((n * per, rows, LANES), jnp.bfloat16),
        ]
        + [dma] * 6,
        compiler_params=pltpu.CompilerParams(
            collective_id=ident, has_side_effects=True, vmem_limit_bytes=16 * 2**20
        ),
    )(values, lse)


def attend_kernel(steps, group, len_ref, q_ref, k_ref, v_ref, nk_ref, nv_ref, o_ref, lse_ref):
    me = lax.axis_index("seq")
    heads, padded, width = q_ref.shape[1:]
    count = k_ref.shape[1]
    fresh_count = nk_ref.shape[2]
    scale = width ** (-0.5)
    fold = q_ref.shape[0]
    place = me * count + lax.broadcasted_iota(jnp.int32, (padded, count), 1)
    row = lax.broadcasted_iota(jnp.int32, (padded, fresh_count), 0)
    slot = lax.broadcasted_iota(jnp.int32, (padded, fresh_count), 1)
    fresh_live = (slot * group <= row) & (slot < steps) & (me == 0)
    across = (((1,), (1,)), ((), ()))
    for c, k in [(c, k) for c in range(fold) for k in range(heads)]:
        live = place < len_ref[pl.program_id(0) * fold + c]
        part = slice(k * width, (k + 1) * width)
        q = q_ref[c, k]
        cached = lax.dot_general(q, k_ref[c, :, part], across, preferred_element_type=jnp.float32)
        fresh = lax.dot_general(q, nk_ref[c, k], across, preferred_element_type=jnp.float32)
        cached = jnp.where(live, cached * scale, NEGATIVE)
        fresh = jnp.where(fresh_live, fresh * scale, NEGATIVE)
        peak = jnp.maximum(
            jnp.max(cached, axis=1, keepdims=True), jnp.max(fresh, axis=1, keepdims=True)
        )
        weight = jnp.where(live, jnp.exp(cached - peak), 0.0)
        weight_fresh = jnp.where(fresh_live, jnp.exp(fresh - peak), 0.0)
        total = jnp.sum(weight, axis=1, keepdims=True) + jnp.sum(
            weight_fresh, axis=1, keepdims=True
        )
        summed = jnp.dot(
            weight.astype(jnp.bfloat16), v_ref[c, :, part], preferred_element_type=jnp.float32
        ) + jnp.dot(
            weight_fresh.astype(jnp.bfloat16), nv_ref[c, k], preferred_element_type=jnp.float32
        )
        safe = jnp.maximum(total, 0.5)
        o_ref[c, k] = (summed / safe).astype(o_ref.dtype)
        log = jnp.where(total > 0.5, peak + jnp.log(safe), NEGATIVE)
        lse_ref[c, k] = jnp.broadcast_to(log, (padded, width))


def attend(query, keys, values, new_keys, new_values, lengths, shards, ident):
    batch, steps, heads, group, width = query.shape
    count = keys.shape[1]
    fold = math.gcd(batch, 4)
    used = steps * group
    padded = -(-used // 16) * 16
    quest = query.transpose(0, 2, 1, 3, 4).reshape(batch, heads, used, width)
    quest = jnp.pad(quest, ((0, 0), (0, 0), (0, padded - used), (0, 0)))

    def slots(new):
        return jnp.pad(new.transpose(0, 2, 1, 3), ((0, 0), (0, 0), (0, -steps % 16), (0, 0)))

    new_keys, new_values = slots(new_keys), slots(new_values)

    def spec(shape):
        return pl.BlockSpec((fold,) + shape, lambda b: (b,) + (0,) * len(shape))

    cache = spec((count, heads * width))
    fresh = spec(new_keys.shape[1:])
    rows_spec = spec((heads, padded, width))
    out, lse = pl.pallas_call(
        functools.partial(attend_kernel, steps, group),
        grid=(batch // fold,),
        out_shape=(
            jax.ShapeDtypeStruct(quest.shape, jnp.bfloat16),
            jax.ShapeDtypeStruct(quest.shape, jnp.float32),
        ),
        in_specs=[
            pl.BlockSpec(memory_space=pltpu.SMEM), rows_spec, cache, cache, fresh, fresh
        ],
        out_specs=(rows_spec, rows_spec),
        compiler_params=pltpu.CompilerParams(vmem_limit_bytes=16 * 2**20),
    )(lengths, quest, keys, values, new_keys, new_values)

    def by_row(x):
        x = x[:, :, :used].reshape(batch, heads, steps, group, -1).transpose(2, 0, 1, 3, 4)
        return x.reshape(steps * batch, -1)

    logs = by_row(lse[..., :1])
    logs = jnp.pad(logs, ((0, 0), (0, LANES - logs.shape[1])))
    return merge_over(by_row(out), logs, shards, ident)


def body(
    thinker_input,
    thinker_gain,
    thinker_qkv,
    thinker_out,
    talker_proj,
    code_table,
    talker_gain,
    talker_qkv,
    talker_out,
    text_keys,
    text_values,
    audio_keys,
    audio_values,
    text_len,
    audio_len,
    text_pos,
    audio_pos,
    code_ids,
):
    steps, batch = thinker_input.shape[:2]
    rows = steps * batch
    index = lax.axis_index("seq")
    shards = lax.axis_size("seq")
    text_kv = HK * HD
    audio_q = AHQ * AHD
    audio_kv = AHK * AHD

    def by_batch(heads):
        return heads.reshape((steps, batch) + heads.shape[1:]).swapaxes(0, 1)

    table_rows = code_table.shape[0]
    table_ids = index * table_rows + jnp.arange(table_rows)
    talker_cols = talker_out.shape[1] // shards
    out_slice = lax.dynamic_slice_in_dim(talker_out, index * talker_cols, talker_cols, 1)
    text_at = text_pos.T.reshape(rows)
    audio_at = audio_pos.T.reshape(rows)
    ids = code_ids.T.reshape(rows)

    inputs = thinker_input.reshape(rows, D).astype(jnp.float32)
    scaled = (inputs * thinker_gain).astype(jnp.bfloat16)
    n = thinker_qkv.shape[0]
    mine = lax.dynamic_slice_in_dim(scaled, index * n, n, 1)
    projected = sum_over(
        jnp.dot(mine, thinker_qkv, preferred_element_type=jnp.float32), shards, 0
    )
    projected = projected * lax.rsqrt(jnp.sum(inputs * inputs, axis=-1) / D + EPSILON)[:, None]
    query = rotate(projected[:, :D].reshape(rows, HQ, HD), text_at).astype(jnp.bfloat16)
    key = rotate(projected[:, D : D + text_kv].reshape(rows, HK, HD), text_at).astype(jnp.bfloat16)
    value = projected[:, D + text_kv :].reshape(rows, HK, HD).astype(jnp.bfloat16)
    attended = attend(
        by_batch(query.reshape(rows, HK, HQ // HK, HD)),
        text_keys,
        text_values,
        by_batch(key),
        by_batch(value),
        text_len,
        shards,
        1,
    )
    n = thinker_out.shape[0]
    mine = lax.dynamic_slice_in_dim(attended, index * n, n, 1)
    contribution = sum_over(
        jnp.dot(mine, thinker_out, preferred_element_type=jnp.float32), shards, 3
    )
    hidden = (inputs + contribution).astype(jnp.bfloat16)
    picked = (ids[:, None] == table_ids[None, :]).astype(jnp.bfloat16)
    n = talker_proj.shape[0]
    mine = lax.dynamic_slice_in_dim(hidden, index * n, n, 1)
    talker_in = sum_over(
        jnp.dot(mine, talker_proj, preferred_element_type=jnp.float32)
        + jnp.dot(picked, code_table, preferred_element_type=jnp.float32),
        shards,
        4,
    )
    normed = (
        talker_in
        * lax.rsqrt(jnp.sum(talker_in * talker_in, axis=-1, keepdims=True) / TD + EPSILON)
        * talker_gain
    ).astype(jnp.bfloat16)
    spoken = jnp.dot(normed, talker_qkv, preferred_element_type=jnp.float32)
    query = rotate(spoken[:, :audio_q].reshape(rows, AHQ, AHD), audio_at).astype(jnp.bfloat16)
    key = rotate(
        spoken[:, audio_q : audio_q + audio_kv].reshape(rows, AHK, AHD), audio_at
    ).astype(jnp.bfloat16)
    value = spoken[:, audio_q + audio_kv :].reshape(rows, AHK, AHD).astype(jnp.bfloat16)
    heard = attend(
        by_batch(query.reshape(rows, AHK, AHQ // AHK, AHD)),
        audio_keys,
        audio_values,
        by_batch(key),
        by_batch(value),
        audio_len,
        shards,
        5,
    )
    residual = lax.dynamic_slice_in_dim(talker_in, index * talker_cols, talker_cols, 1)
    spoken_out = residual + jnp.dot(heard, out_slice, preferred_element_type=jnp.float32)
    return (
        hidden.reshape(steps, batch, D),
        spoken_out.astype(jnp.bfloat16).reshape(steps, batch, talker_cols),
    )


def solution(mesh):
    return jax.shard_map(
        body,
        mesh=mesh,
        in_specs=(
            P(None, "grp", None),
            P(),
            P("seq", None),
            P("seq", None),
            P("seq", None),
            P("seq", None),
            P(),
            P(),
            P(),
            P("grp", "seq", None),
            P("grp", "seq", None),
            P("grp", "seq", None),
            P("grp", "seq", None),
            P("grp"),
            P("grp"),
            P("grp", None),
            P("grp", None),
            P("grp", None),
        ),
        out_specs=(P(None, "grp", None), P(None, "grp", "seq")),
        check_vma=False,
    )
```
